512 devices in a mesh: ctx: 64 (over y, z), head: 8 (over x, core).
Axes of the slice: x: 4, y: 4, z: 16, core: 2. Of those that a mesh axis runs over, the one named last changes fastest.
Arguments:
- query_rows: bfloat16 [8, 65536, 8, 128], P('head', 'ctx'), may hold values from -64 to 64
- key_rows: bfloat16 [8, 262144, 128], P('head', 'ctx'), may hold values from -80 to 80
- value_rows: bfloat16 [8, 262144, 128], P('head', 'ctx'), may hold values from -20 to 20
Outputs:
- key_scores: float32 [8, 262144], P('head', 'ctx')
The draws below stay inside these ranges and needn't reach their ends.
All inputs are finite; a program needn't handle non-finite values.
Results may differ from the reference program's by a relative error of at most 0.0003.
Values may be sent and summed in bfloat16 or wider, within the bound.
A program may use at most 128 MiB of HBM per device.

```python
import math
import jax
import jax.numpy as jnp
from jax import lax

DH = 128
KVH = 8
REP = 8
KTOKENS = 262144
QTOKENS = 65536


def draw_query_rows(key, part):
    key = jax.random.fold_in(key, 11)
    keys_list = jax.random.split(key, 3)
    center = jax.random.normal(keys_list[0], (REP, 1, KVH, DH), jnp.float32) * 0.6
    spread = jnp.exp(jax.random.uniform(keys_list[1], (REP, 1, KVH, DH), jnp.float32, math.log(0.3), math.log(3.0)))
    noise = jax.random.normal(keys_list[2], (REP, QTOKENS, KVH, DH), jnp.float32)
    mixed = spread * noise + 0.5 * spread * jnp.roll(noise, 1, axis=3)
    return jnp.clip(center + mixed, -64.0, 64.0).astype(jnp.bfloat16)


def draw_key_rows(key, part):
    key = jax.random.fold_in(key, 23)
    keys_list = jax.random.split(key, 1)
    base = jnp.clip(jax.random.normal(keys_list[0], (KVH, KTOKENS, DH), jnp.float32), -6.0, 6.0)
    return base.astype(jnp.bfloat16)


def draw_value_rows(key, part):
    key = jax.random.fold_in(key, 37)
    keys_list = jax.random.split(key, 2)
    scale = jnp.exp(jax.random.uniform(keys_list[0], (KVH, KTOKENS, 1), jnp.float32, math.log(0.3), math.log(3.0)))
    noise = jnp.clip(jax.random.normal(keys_list[1], (KVH, KTOKENS, DH), jnp.float32), -6.0, 6.0)
    return (scale * noise).astype(jnp.bfloat16)


def setup_inputs(seed: int = 0) -> dict:
    splits = jax.random.split(jax.random.key(seed), 4)
    query_rows = draw_query_rows(jax.random.fold_in(splits[3], 71), 0)
    key_rows = draw_key_rows(jax.random.fold_in(splits[3], 71), 0)
    value_rows = draw_value_rows(jax.random.fold_in(splits[3], 71), 0)
    return dict(query_rows=query_rows, key_rows=key_rows, value_rows=value_rows)


def reference(query_rows, key_rows, value_rows):

    def moments(head_rows):
        query_float = head_rows.astype(jnp.float32)
        second = jnp.einsum('tgd,tge->gde', query_float, query_float, precision=lax.Precision.HIGHEST)
        return (second, lax.optimization_barrier(jnp.sum(query_float, axis=0)))
    moment_two, moment_one = lax.map(moments, query_rows)
    center = moment_one / QTOKENS
    covariance = moment_two / QTOKENS - center[..., :, None] * center[..., None, :]

    def per_group(items):
        group_keys, group_values, group_cov, group_center = items
        key_float = group_keys.astype(jnp.float32)

        def per_head(pair):
            matrix, vector = pair
            projected = jnp.dot(key_float, matrix, precision=lax.Precision.HIGHEST)
            quadratic = lax.optimization_barrier(jnp.sum(projected * key_float, axis=-1))
            linear = jnp.dot(key_float, vector, precision=lax.Precision.HIGHEST)
            return linear / math.sqrt(DH) + quadratic / (2.0 * DH)
        exponent = lax.map(per_head, (group_cov, group_center))
        highest = lax.optimization_barrier(jnp.max(exponent, axis=-1, keepdims=True))
        mass = lax.optimization_barrier(jnp.sum(jnp.exp(exponent - highest), axis=-1, keepdims=True))
        share = lax.optimization_barrier(jnp.sum(jnp.exp(exponent - highest) / mass, axis=0))
        value_float = group_values.astype(jnp.float32)
        value_scale = jnp.sqrt(lax.optimization_barrier(jnp.sum(value_float * value_float, axis=-1)) / DH + 1e-06)
        return share * value_scale
    weighted = lax.map(per_group, (key_rows, value_rows, jnp.swapaxes(covariance, 0, 1), jnp.swapaxes(center, 0, 1)))
    return KTOKENS / REP * weighted
```

```python
import functools
import math

import jax
import jax.numpy as jnp
from jax import lax
from jax.experimental import pallas as pl
from jax.experimental.pallas import tpu as pltpu
from jax.sharding import PartitionSpec as P

MESH = pl.DeviceIdType.MESH
F32 = jnp.float32
BF16 = jnp.bfloat16

NY, NZ, NH = 4, 16, 8
DH = 128
HALF = DH // 2
REP = 8
ROWS = 9
FAR_FIRST = (8, 7, 9, 6, 10, 5, 11, 4, 12, 3, 13, 2, 14, 1, 15)


def split_two(value):
    high = value.astype(BF16)
    low = (value - high.astype(F32)).astype(BF16)
    return high, low


def kernel(
    query_count, key_count,
    q_hbm, k_hbm, v_hbm, out_ref,
    q_in, k_in, v_in, q_f32, packed, plane, line, part, full, weights, keys_t, scale,
    expo, mass, in_sem, send_sem, recv_sem,
):
    ctx = lax.axis_index("ctx")
    head = lax.axis_index("head")
    y = lax.div(ctx, NZ)
    z = lax.rem(ctx, NZ)

    load_q = pltpu.make_async_copy(q_hbm, q_in, in_sem.at[0])
    load_k = pltpu.make_async_copy(k_hbm, k_in, in_sem.at[1])
    load_v = pltpu.make_async_copy(v_hbm, v_in, in_sem.at[2])
    load_q.start()
    load_k.start()
    load_v.start()

    plane_peers = [
        (lax.rem(y + dy, NY), lax.rem(head + dh, NH))
        for dy in range(NY)
        for dh in range(NH)
        if (dy, dh) != (0, 0)
    ]
    line_peers = [lax.rem(z + dz, NZ) for dz in FAR_FIRST]

    barrier = pltpu.get_barrier_semaphore()
    for zz in line_peers:
        pl.semaphore_signal(barrier, inc=1, device_id=(y * NZ + zz, head), device_id_type=MESH)
    for yy, hh in plane_peers:
        pl.semaphore_signal(barrier, inc=1, device_id=(yy * NZ + z, hh), device_id_type=MESH)

    load_q.wait()
    step = 64

    def widen(t, _):
        rows = q_in[0, pl.ds(t * step, step)].astype(F32)
        q_f32[pl.ds(t * step * NH, step * NH), :] = rows.reshape(step * NH, DH)
        return 0

    lax.fori_loop(0, query_count // step, widen, 0)
    row = lax.broadcasted_iota(jnp.int32, (HALF, DH), 0)
    lane = lax.broadcasted_iota(jnp.int32, (HALF, DH), 1)
    for g in range(NH):
        rows = q_f32[pl.ds(g, query_count, stride=NH), :]
        first = jnp.sum(rows, axis=0, keepdims=True)
        narrow = rows.astype(BF16)
        second = lax.dot_general(
            narrow, narrow, (((0,), (0,)), ((), ())), preferred_element_type=F32
        )
        top = second[:HALF]
        bottom = pltpu.roll(second[HALF:], HALF, 1)
        both = jnp.where(lane < row, bottom, top)
        diagonal = jnp.sum(jnp.where(lane == row, bottom, 0.0), axis=0, keepdims=True)
        for q in range(NY):
            for h in range(2):
                at = q * 16 + h * 8
                packed[g, q, h, 0:8, :] = both[at : at + 8]
            packed[g, q, 0, 8:9, :] = first
            packed[g, q, 1, 8:9, :] = diagonal

    pl.semaphore_wait(barrier, len(plane_peers) + len(line_peers))

    def copy(src, dst, phase, device):
        return pltpu.make_async_remote_copy(
            src_ref=src, dst_ref=dst, send_sem=send_sem.at[phase], recv_sem=recv_sem.at[phase],
            device_id=device, device_id_type=MESH,
        )

    def wait(ref, sem):
        pltpu.make_async_copy(ref, ref, sem).wait()

    for yy, hh in plane_peers:
        copy(
            packed.at[hh, yy, :, pl.ds(0, ROWS)],
            plane.at[pl.ds(y * 16 + 2 * head, 2), pl.ds(0, ROWS)],
            0, (yy * NZ + z, hh),
        ).start()
    plane[pl.ds(y * 16 + 2 * head, 2), 0:ROWS, :] = packed[head, y, :, 0:ROWS, :]

    load_k.wait()
    wide = 512

    def turn_keys(t, _):
        turned = k_in[0, pl.ds(t * wide, wide), :].astype(F32).T.astype(BF16)
        keys_t[0:DH, pl.ds(t * wide, wide)] = turned
        keys_t[DH : 2 * DH, pl.ds(t * wide, wide)] = turned
        return 0

    lax.fori_loop(0, key_count // wide, turn_keys, 0)

    wait(plane.at[pl.ds(0, 62), pl.ds(0, ROWS)], recv_sem.at[0])
    total = plane[0:16, 0:ROWS, :]
    for yy in range(1, NY):
        total = total + plane[yy * 16 : yy * 16 + 16, 0:ROWS, :]
    line[:, 0:ROWS, :] = total

    for zz in line_peers:
        copy(line.at[zz, pl.ds(0, ROWS)], part.at[z, pl.ds(0, ROWS)], 1, (y * NZ + zz, head)).start()
    part[z, 0:ROWS, :] = line[z, 0:ROWS, :]

    load_v.wait()

    def scale_values(t, _):
        turned = v_in[0, pl.ds(t * wide, wide), :].astype(F32).T
        squares = jnp.sum(turned * turned, axis=0, keepdims=True)
        scale[:, pl.ds(t * wide, wide)] = jnp.sqrt(squares / DH + 1e-06)
        return 0

    lax.fori_loop(0, key_count // wide, scale_values, 0)

    wait(part.at[pl.ds(0, 15), pl.ds(0, ROWS)], recv_sem.at[1])
    total = part[0, 0:ROWS, :]
    for zz in range(1, NZ):
        total = total + part[zz, 0:ROWS, :]
    mine = y * 16 + z
    full[mine, 0:ROWS, :] = total

    for zz in line_peers:
        here = full.at[mine, pl.ds(0, ROWS)]
        copy(here, here, 2, (y * NZ + zz, head)).start()
    wait(full.at[pl.ds(0, 15), pl.ds(0, ROWS)], recv_sem.at[2])

    for dy in range(1, NY):
        here = full.at[pl.ds(y * 16, 16), pl.ds(0, 8)]
        copy(here, here, 3, (lax.rem(y + dy, NY) * NZ + z, head)).start()
    extra = full[pl.ds(y * 16, 16), 8, :] * (1.0 / (query_count * NY * NZ))
    columns = extra.T
    wait(full.at[pl.ds(0, 48), pl.ds(0, 8)], recv_sem.at[3])

    for r in range(REP):
        quarters = [full[q * 16 + 2 * r + h, 0:8, :] for q in range(NY) for h in range(2)]
        moments = jnp.concatenate(quarters, axis=0) * (1.0 / (query_count * NY * NZ))
        center = extra[2 * r : 2 * r + 1, :]
        up = columns[0:HALF, 2 * r : 2 * r + 1]
        down = columns[HALF:DH, 2 * r : 2 * r + 1]
        diagonal = columns[0:HALF, 2 * r + 1 : 2 * r + 2]
        below = lane < row
        value = moments - jnp.where(below, down * pltpu.roll(center, HALF, 1), up * center)
        value = value * (1.0 / (2.0 * DH))
        corner = (diagonal - down * down) * (1.0 / (2.0 * DH))
        on = lane == row
        upper = jnp.where(below, 0.0, jnp.where(on, value, 2.0 * value))
        lower = jnp.where(below, 2.0 * value, jnp.where(on, corner, 0.0))
        for at, block in ((0, upper), (HALF, pltpu.roll(lower, HALF, 1))):
            high, low = split_two(block)
            weights[r * DH + at : r * DH + at + HALF, 0:DH] = high
            weights[r * DH + at : r * DH + at + HALF, DH : 2 * DH] = low
    high, low = split_two(extra * (1.0 / math.sqrt(DH)))
    weights[REP * DH : REP * DH + 16, 0:DH] = high
    weights[REP * DH : REP * DH + 16, DH : 2 * DH] = low

    tile = 256

    def score(t, _):
        keys = keys_t[:, pl.ds(t * tile, tile)]
        keys_f32 = keys[0:DH].astype(F32)
        projected = jnp.dot(weights[...], keys, preferred_element_type=F32)
        for r in range(REP):
            quadratic = jnp.sum(projected[r * DH : (r + 1) * DH] * keys_f32, axis=0, keepdims=True)
            linear = projected[REP * DH + 2 * r : REP * DH + 2 * r + 1]
            expo[r : r + 1, pl.ds(t * tile, tile)] = quadratic + linear
        return 0

    lax.fori_loop(0, key_count // tile, score, 0)

    exponent = expo[...]
    peak = jnp.max(exponent, axis=1, keepdims=True)
    grown = jnp.exp(exponent - peak)
    expo[...] = grown
    local = jnp.sum(grown, axis=1, keepdims=True)
    row8 = lax.broadcasted_iota(jnp.int32, (REP, DH), 0)
    lane8 = lax.broadcasted_iota(jnp.int32, (REP, DH), 1)
    note = jnp.where(lane8 == row8, peak, jnp.where(lane8 == row8 + REP, local, 0.0))
    mass[pl.ds(ctx, 1), :] = jnp.sum(note, axis=0, keepdims=True)
    for dz in FAR_FIRST + (0,):
        for dy in (2, 1, 3, 0):
            if (dy, dz) != (0, 0):
                here = mass.at[pl.ds(ctx, 1)]
                copy(here, here, 4, (lax.rem(y + dy, NY) * NZ + lax.rem(z + dz, NZ), head)).start()
    wait(mass.at[pl.ds(0, 63)], recv_sem.at[4])
    notes = mass[...]
    highest = jnp.max(notes, axis=0, keepdims=True)
    sums = pltpu.roll(notes, DH - REP, 1)
    inside = lax.broadcasted_iota(jnp.int32, notes.shape, 1) < REP
    terms = jnp.where(inside, sums * jnp.exp(jnp.where(inside, notes - highest, 0.0)), 0.0)
    denominator = jnp.sum(terms, axis=0, keepdims=True)
    pick = lane8 == row8
    highest_col = jnp.sum(jnp.where(pick, highest, 0.0), axis=1, keepdims=True)
    denominator_col = jnp.sum(jnp.where(pick, denominator, 0.0), axis=1, keepdims=True)
    factor = jnp.exp(peak - highest_col) / denominator_col
    share = jnp.sum(expo[...] * factor, axis=0, keepdims=True)
    out_ref[...] = share * scale[...] * (key_count * NY * NZ / REP)

    wait(plane.at[pl.ds(0, 62), pl.ds(0, ROWS)], send_sem.at[0])
    wait(part.at[pl.ds(0, 15), pl.ds(0, ROWS)], send_sem.at[1])
    wait(full.at[pl.ds(0, 15), pl.ds(0, ROWS)], send_sem.at[2])
    wait(full.at[pl.ds(0, 48), pl.ds(0, 8)], send_sem.at[3])
    wait(mass.at[pl.ds(0, 63)], send_sem.at[4])


def local(query_rows, key_rows, value_rows):
    query_count = query_rows.shape[1]
    key_count = key_rows.shape[1]
    any_space = pl.BlockSpec(memory_space=pl.ANY)
    return pl.pallas_call(
        functools.partial(kernel, query_count, key_count),
        out_shape=jax.ShapeDtypeStruct((1, key_count), F32),
        in_specs=[any_space] * 3,
        out_specs=pl.BlockSpec(memory_space=pltpu.VMEM),
        scratch_shapes=[
            pltpu.VMEM(query_rows.shape, BF16),
            pltpu.VMEM(key_rows.shape, BF16),
            pltpu.VMEM(value_rows.shape, BF16),
            pltpu.VMEM((query_count * NH, DH), F32),
            pltpu.VMEM((NH, NY, 2, 16, DH), F32),
            pltpu.VMEM((NY * 16, 16, DH), F32),
            pltpu.VMEM((NZ, 16, DH), F32),
            pltpu.VMEM((NZ, 16, DH), F32),
            pltpu.VMEM((NY * 16, 16, DH), F32),
            pltpu.VMEM((REP * DH + 16, 2 * DH), BF16),
            pltpu.VMEM((2 * DH, key_count), BF16),
            pltpu.VMEM((1, key_count), F32),
            pltpu.VMEM((REP, key_count), F32),
            pltpu.VMEM((NY * NZ, DH), F32),
            pltpu.SemaphoreType.DMA((3,)),
            pltpu.SemaphoreType.DMA((5,)),
            pltpu.SemaphoreType.DMA((5,)),
        ],
        compiler_params=pltpu.CompilerParams(
            collective_id=0, has_side_effects=True, vmem_limit_bytes=48 << 20
        ),
    )(query_rows, key_rows, value_rows)


def solution(mesh):
    in_specs = (P("head", "ctx", None, None), P("head", "ctx", None), P("head", "ctx", None))
    return jax.shard_map(
        local, mesh=mesh, in_specs=in_specs, out_specs=P("head", "ctx"), check_vma=False
    )
```

```python
import functools
import math

import jax
import jax.numpy as jnp
from jax import lax
from jax.experimental import pallas as pl
from jax.experimental.pallas import tpu as pltpu
from jax.sharding import PartitionSpec as P

MESH = pl.DeviceIdType.MESH
F32 = jnp.float32
BF16 = jnp.bfloat16

NY, NZ, NH = 4, 16, 8
DH = 128
HALF = DH // 2
REP = 8
ROWS = 9
FAR_FIRST = (8, 7, 9, 6, 10, 5, 11, 4, 12, 3, 13, 2, 14, 1, 15)
PLANE = sorted(
    ((dy, dx) for dy in range(4) for dx in range(4)),
    key=lambda d: -(min(d[0], 4 - d[0]) + min(d[1], 4 - d[1])),
)


def split_two(value):
    high = value.astype(BF16)
    low = (value - high.astype(F32)).astype(BF16)
    return high, low


def kernel(
    query_count, key_count,
    q_hbm, k_hbm, v_hbm, out_ref,
    q_in, k_in, v_in, q_f32, packed, plane, line, part, full, weights, keys_t, scale,
    expo, mass, in_sem, send_sem, recv_sem, told,
):
    ctx = lax.axis_index("ctx")
    head = lax.axis_index("head")
    y = lax.div(ctx, NZ)
    z = lax.rem(ctx, NZ)

    load_q = pltpu.make_async_copy(q_hbm, q_in, in_sem.at[0])
    load_k = pltpu.make_async_copy(k_hbm, k_in, in_sem.at[1])
    load_v = pltpu.make_async_copy(v_hbm, v_in, in_sem.at[2])
    load_q.start()

    plane_peers = [
        (lax.rem(y + dy, NY), lax.rem(head + 2 * dx + dc, NH))
        for dy, dx in PLANE
        for dc in range(2)
        if (dy, dx, dc) != (0, 0, 0)
    ]
    line_peers = [lax.rem(z + dz, NZ) for dz in FAR_FIRST]

    barrier = pltpu.get_barrier_semaphore()
    core = lax.rem(head, 2)
    even = head - core
    odd = even + 1

    def greet(device):
        pl.semaphore_signal(barrier, inc=1, device_id=device, device_id_type=MESH)

    for dy, dx in PLANE:
        if (dy, dx) != (0, 0):
            greet((lax.rem(y + dy, NY) * NZ + z, lax.rem(odd + 2 * dx, NH)))
    for zz in line_peers:
        greet((y * NZ + zz, even))

    @pl.when(core == 0)
    def _():
        greet((ctx, odd))

    load_q.wait()
    load_k.start()
    load_v.start()
    step = 64

    def widen(t, _):
        rows = q_in[0, pl.ds(t * step, step)].astype(F32)
        q_f32[pl.ds(t * step * NH, step * NH), :] = rows.reshape(step * NH, DH)
        return 0

    lax.fori_loop(0, query_count // step, widen, 0)
    row = lax.broadcasted_iota(jnp.int32, (HALF, DH), 0)
    lane = lax.broadcasted_iota(jnp.int32, (HALF, DH), 1)
    for g in range(NH):
        rows = q_f32[pl.ds(g, query_count, stride=NH), :]
        first = jnp.sum(rows, axis=0, keepdims=True)
        narrow = rows.astype(BF16)
        second = lax.dot_general(
            narrow, narrow, (((0,), (0,)), ((), ())), preferred_element_type=F32
        )
        top = second[:HALF]
        bottom = pltpu.roll(second[HALF:], HALF, 1)
        both = jnp.where(lane < row, bottom, top)
        diagonal = jnp.sum(jnp.where(lane == row, bottom, 0.0), axis=0, keepdims=True)
        for q in range(NY):
            for h in range(2):
                at = q * 16 + h * 8
                packed[g, q, h, 0:8, :] = both[at : at + 8]
            packed[g, q, 0, 8:9, :] = first
            packed[g, q, 1, 8:9, :] = diagonal

    @pl.when(core == 1)
    def _():
        pl.semaphore_wait(barrier, 31)
        pl.semaphore_signal(told, inc=1, device_id=(ctx, even), device_id_type=MESH)

    @pl.when(core == 0)
    def _():
        pl.semaphore_wait(told, 1)

    def copy(src, dst, phase, device):
        return pltpu.make_async_remote_copy(
            src_ref=src, dst_ref=dst, send_sem=send_sem.at[phase], recv_sem=recv_sem.at[phase],
            device_id=device, device_id_type=MESH,
        )

    def wait(ref, sem):
        pltpu.make_async_copy(ref, ref, sem).wait()

    for yy, hh in plane_peers:
        copy(
            packed.at[hh, yy, :, pl.ds(0, ROWS)],
            plane.at[pl.ds(y * 16 + 2 * head, 2), pl.ds(0, ROWS)],
            0, (yy * NZ + z, hh),
        ).start()
    plane[pl.ds(y * 16 + 2 * head, 2), 0:ROWS, :] = packed[head, y, :, 0:ROWS, :]

    load_k.wait()
    wide = 512

    def turn_keys(t, _):
        turned = k_in[0, pl.ds(t * wide, wide), :].astype(F32).T.astype(BF16)
        keys_t[0:DH, pl.ds(t * wide, wide)] = turned
        keys_t[DH : 2 * DH, pl.ds(t * wide, wide)] = turned
        return 0

    lax.fori_loop(0, key_count // wide, turn_keys, 0)

    @pl.when(core == 0)
    def _():
        pl.semaphore_wait(barrier, 30)
        pl.semaphore_signal(told, inc=1, device_id=(ctx, odd), device_id_type=MESH)

    wait(plane.at[pl.ds(0, 62), pl.ds(0, ROWS)], recv_sem.at[0])
    total = plane[0:16, 0:ROWS, :]
    for yy in range(1, NY):
        total = total + plane[yy * 16 : yy * 16 + 16, 0:ROWS, :]
    line[:, 0:ROWS, :] = total

    @pl.when(core == 1)
    def _():
        pl.semaphore_wait(told, 1)

    for zz in line_peers:
        copy(line.at[zz, pl.ds(0, ROWS)], part.at[z, pl.ds(0, ROWS)], 1, (y * NZ + zz, head)).start()
    part[z, 0:ROWS, :] = line[z, 0:ROWS, :]

    load_v.wait()

    def scale_values(t, _):
        turned = v_in[0, pl.ds(t * wide, wide), :].astype(F32).T
        squares = jnp.sum(turned * turned, axis=0, keepdims=True)
        scale[:, pl.ds(t * wide, wide)] = jnp.sqrt(squares / DH + 1e-06)
        return 0

    lax.fori_loop(0, key_count // wide, scale_values, 0)

    wait(part.at[pl.ds(0, 15), pl.ds(0, ROWS)], recv_sem.at[1])
    total = part[0, 0:ROWS, :]
    for zz in range(1, NZ):
        total = total + part[zz, 0:ROWS, :]
    mine = y * 16 + z
    full[mine, 0:ROWS, :] = total

    for zz in line_peers:
        here = full.at[mine, pl.ds(0, ROWS)]
        copy(here, here, 2, (y * NZ + zz, head)).start()
    wait(full.at[pl.ds(0, 15), pl.ds(0, ROWS)], recv_sem.at[2])

    for dy in range(1, NY):
        here = full.at[pl.ds(y * 16, 16), pl.ds(0, 8)]
        copy(here, here, 3, (lax.rem(y + dy, NY) * NZ + z, head)).start()
    extra = full[pl.ds(y * 16, 16), 8, :] * (1.0 / (query_count * NY * NZ))
    columns = extra.T
    wait(full.at[pl.ds(0, 48), pl.ds(0, 8)], recv_sem.at[3])

    for r in range(REP):
        quarters = [full[q * 16 + 2 * r + h, 0:8, :] for q in range(NY) for h in range(2)]
        moments = jnp.concatenate(quarters, axis=0) * (1.0 / (query_count * NY * NZ))
        center = extra[2 * r : 2 * r + 1, :]
        up = columns[0:HALF, 2 * r : 2 * r + 1]
        down = columns[HALF:DH, 2 * r : 2 * r + 1]
        diagonal = columns[0:HALF, 2 * r + 1 : 2 * r + 2]
        below = lane < row
        value = moments - jnp.where(below, down * pltpu.roll(center, HALF, 1), up * center)
        value = value * (1.0 / (2.0 * DH))
        corner = (diagonal - down * down) * (1.0 / (2.0 * DH))
        on = lane == row
        upper = jnp.where(below, 0.0, jnp.where(on, value, 2.0 * value))
        lower = jnp.where(below, 2.0 * value, jnp.where(on, corner, 0.0))
        for at, block in ((0, upper), (HALF, pltpu.roll(lower, HALF, 1))):
            high, low = split_two(block)
            weights[r * DH + at : r * DH + at + HALF, 0:DH] = high
            weights[r * DH + at : r * DH + at + HALF, DH : 2 * DH] = low
    high, low = split_two(extra * (1.0 / math.sqrt(DH)))
    weights[REP * DH : REP * DH + 16, 0:DH] = high
    weights[REP * DH : REP * DH + 16, DH : 2 * DH] = low

    tile = 512
    for t in range(key_count // tile):
        keys = keys_t[:, t * tile : (t + 1) * tile]
        keys_f32 = keys[0:DH].astype(F32)
        projected = jnp.dot(weights[...], keys, preferred_element_type=F32)
        for r in range(REP):
            quadratic = jnp.sum(projected[r * DH : (r + 1) * DH] * keys_f32, axis=0, keepdims=True)
            linear = projected[REP * DH + 2 * r : REP * DH + 2 * r + 1]
            expo[r : r + 1, t * tile : (t + 1) * tile] = quadratic + linear

    exponent = expo[...]
    peak = jnp.max(exponent, axis=1, keepdims=True)
    grown = jnp.exp(exponent - peak)
    expo[...] = grown
    local = jnp.sum(grown, axis=1, keepdims=True)
    row8 = lax.broadcasted_iota(jnp.int32, (REP, DH), 0)
    lane8 = lax.broadcasted_iota(jnp.int32, (REP, DH), 1)
    note = jnp.where(lane8 == row8, peak, jnp.where(lane8 == row8 + REP, local, 0.0))
    mass[pl.ds(ctx, 1), :] = jnp.sum(note, axis=0, keepdims=True)
    for dz in FAR_FIRST + (0,):
        for dy in (2, 1, 3, 0):
            if (dy, dz) != (0, 0):
                here = mass.at[pl.ds(ctx, 1)]
                copy(here, here, 4, (lax.rem(y + dy, NY) * NZ + lax.rem(z + dz, NZ), head)).start()
    wait(mass.at[pl.ds(0, 63)], recv_sem.at[4])
    notes = mass[...]
    highest = jnp.max(notes, axis=0, keepdims=True)
    sums = pltpu.roll(notes, DH - REP, 1)
    inside = lax.broadcasted_iota(jnp.int32, notes.shape, 1) < REP
    terms = jnp.where(inside, sums * jnp.exp(jnp.where(inside, notes - highest, 0.0)), 0.0)
    denominator = jnp.sum(terms, axis=0, keepdims=True)
    pick = lane8 == row8
    highest_col = jnp.sum(jnp.where(pick, highest, 0.0), axis=1, keepdims=True)
    denominator_col = jnp.sum(jnp.where(pick, denominator, 0.0), axis=1, keepdims=True)
    factor = jnp.exp(peak - highest_col) / denominator_col
    share = jnp.sum(expo[...] * factor, axis=0, keepdims=True)
    out_ref[...] = share * scale[...] * (key_count * NY * NZ / REP)

    wait(plane.at[pl.ds(0, 62), pl.ds(0, ROWS)], send_sem.at[0])
    wait(part.at[pl.ds(0, 15), pl.ds(0, ROWS)], send_sem.at[1])
    wait(full.at[pl.ds(0, 15), pl.ds(0, ROWS)], send_sem.at[2])
    wait(full.at[pl.ds(0, 48), pl.ds(0, 8)], send_sem.at[3])
    wait(mass.at[pl.ds(0, 63)], send_sem.at[4])


def local(query_rows, key_rows, value_rows):
    query_count = query_rows.shape[1]
    key_count = key_rows.shape[1]
    any_space = pl.BlockSpec(memory_space=pltpu.HBM)
    return pl.pallas_call(
        functools.partial(kernel, query_count, key_count),
        out_shape=jax.ShapeDtypeStruct((1, key_count), F32),
        in_specs=[any_space] * 3,
        out_specs=pl.BlockSpec(memory_space=pltpu.VMEM),
        scratch_shapes=[
            pltpu.VMEM(query_rows.shape, BF16),
            pltpu.VMEM(key_rows.shape, BF16),
            pltpu.VMEM(value_rows.shape, BF16),
            pltpu.VMEM((query_count * NH, DH), F32),
            pltpu.VMEM((NH, NY, 2, 16, DH), F32),
            pltpu.VMEM((NY * 16, 16, DH), F32),
            pltpu.VMEM((NZ, 16, DH), F32),
            pltpu.VMEM((NZ, 16, DH), F32),
            pltpu.VMEM((NY * 16, 16, DH), F32),
            pltpu.VMEM((REP * DH + 16, 2 * DH), BF16),
            pltpu.VMEM((2 * DH, key_count), BF16),
            pltpu.VMEM((1, key_count), F32),
            pltpu.VMEM((REP, key_count), F32),
            pltpu.VMEM((NY * NZ, DH), F32),
            pltpu.SemaphoreType.DMA((3,)),
            pltpu.SemaphoreType.DMA((5,)),
            pltpu.SemaphoreType.DMA((5,)),
            pltpu.SemaphoreType.REGULAR,
        ],
        compiler_params=pltpu.CompilerParams(
            collective_id=0, has_side_effects=True, vmem_limit_bytes=62 << 20
        ),
    )(query_rows, key_rows, value_rows)


def solution(mesh):
    in_specs = (P("head", "ctx", None, None), P("head", "ctx", None), P("head", "ctx", None))
    return jax.shard_map(
        local, mesh=mesh, in_specs=in_specs, out_specs=P("head", "ctx"), check_vma=False
    )
```

```python
import functools
import math

import jax
import jax.numpy as jnp
from jax import lax
from jax.experimental import pallas as pl
from jax.experimental.pallas import tpu as pltpu
from jax.sharding import PartitionSpec as P

MESH = pl.DeviceIdType.MESH
F32 = jnp.float32
BF16 = jnp.bfloat16

NY, NZ, NH = 4, 16, 8
DH = 128
HALF = DH // 2
REP = 8
ROWS = 9
FAR_FIRST = (8, 7, 9, 6, 10, 5, 11, 4, 12, 3, 13, 2, 14, 1, 15)
FAR = (8, 7, 9, 6, 10)
NEAR = (5, 11, 4, 12, 3, 13, 2, 14, 1, 15)
ORDER = (0, 1, 2, 6, 7, 3, 4, 5)
PLANE = sorted(
    ((dy, dx) for dy in range(4) for dx in range(4)),
    key=lambda d: -(min(d[0], 4 - d[0]) + min(d[1], 4 - d[1])),
)


def split_two(value):
    high = value.astype(BF16)
    low = (value - high.astype(F32)).astype(BF16)
    return high, low


def kernel(
    query_count, key_count,
    q_hbm, k_hbm, v_hbm, out_ref,
    q_in, k_in, v_in, q_f32, packed, plane, line, part, full, weights, keys_t, scale,
    expo, mass, in_sem, send_sem, recv_sem, told,
):
    ctx = lax.axis_index("ctx")
    head = lax.axis_index("head")
    y = lax.div(ctx, NZ)
    z = lax.rem(ctx, NZ)

    load_q = pltpu.make_async_copy(q_hbm, q_in, in_sem.at[0])
    load_k = pltpu.make_async_copy(k_hbm, k_in, in_sem.at[1])
    load_v = pltpu.make_async_copy(v_hbm, v_in, in_sem.at[2])
    load_q.start()

    plane_peers = [
        (lax.rem(y + dy, NY), lax.rem(head + 2 * dx + dc, NH))
        for dy, dx in PLANE
        for dc in range(2)
        if (dy, dx, dc) != (0, 0, 0)
    ]
    line_peers = [lax.rem(z + dz, NZ) for dz in FAR_FIRST]

    barrier = pltpu.get_barrier_semaphore()
    core = lax.rem(head, 2)
    even = head - core
    odd = even + 1

    def greet(device):
        pl.semaphore_signal(barrier, inc=1, device_id=device, device_id_type=MESH)

    for dy, dx in PLANE:
        if (dy, dx) != (0, 0):
            greet((lax.rem(y + dy, NY) * NZ + z, lax.rem(odd + 2 * dx, NH)))
    for zz in line_peers:
        greet((y * NZ + zz, even))

    @pl.when(core == 0)
    def _():
        greet((ctx, odd))

    load_q.wait()
    load_k.start()
    load_v.start()
    step = 64

    def widen(t, _):
        rows = q_in[0, pl.ds(t * step, step)].astype(F32)
        q_f32[pl.ds(t * step * NH, step * NH), :] = rows.reshape(step * NH, DH)
        return 0

    lax.fori_loop(0, query_count // step, widen, 0)
    row = lax.broadcasted_iota(jnp.int32, (HALF, DH), 0)
    lane = lax.broadcasted_iota(jnp.int32, (HALF, DH), 1)
    for g in range(NH):
        rows = q_f32[pl.ds(g, query_count, stride=NH), :]
        first = jnp.sum(rows, axis=0, keepdims=True)
        narrow = rows.astype(BF16)
        second = lax.dot_general(
            narrow, narrow, (((0,), (0,)), ((), ())), preferred_element_type=F32
        )
        top = second[:HALF]
        bottom = pltpu.roll(second[HALF:], HALF, 1)
        both = jnp.where(lane < row, bottom, top)
        diagonal = jnp.sum(jnp.where(lane == row, bottom, 0.0), axis=0, keepdims=True)
        for q in range(NY):
            for h in range(2):
                at = q * 16 + h * 8
                packed[g, q, h, 0:8, :] = both[at : at + 8]
            packed[g, q, 0, 8:9, :] = first
            packed[g, q, 1, 8:9, :] = diagonal

    @pl.when(core == 1)
    def _():
        pl.semaphore_wait(barrier, 31)
        pl.semaphore_signal(told, inc=1, device_id=(ctx, even), device_id_type=MESH)

    @pl.when(core == 0)
    def _():
        pl.semaphore_wait(told, 1)

    def copy(src, dst, phase, device):
        return pltpu.make_async_remote_copy(
            src_ref=src, dst_ref=dst, send_sem=send_sem.at[phase], recv_sem=recv_sem.at[phase],
            device_id=device, device_id_type=MESH,
        )

    def wait(ref, sem):
        pltpu.make_async_copy(ref, ref, sem).wait()

    for yy, hh in plane_peers:
        copy(
            packed.at[hh, yy, :, pl.ds(0, ROWS)],
            plane.at[pl.ds(y * 16 + 2 * head, 2), pl.ds(0, ROWS)],
            0, (yy * NZ + z, hh),
        ).start()
    plane[pl.ds(y * 16 + 2 * head, 2), 0:ROWS, :] = packed[head, y, :, 0:ROWS, :]

    load_k.wait()
    wide = 512

    def turn_keys(t, _):
        turned = k_in[0, pl.ds(t * wide, wide), :].astype(F32).T.astype(BF16)
        keys_t[0:DH, pl.ds(t * wide, wide)] = turned
        keys_t[DH : 2 * DH, pl.ds(t * wide, wide)] = turned
        return 0

    lax.fori_loop(0, key_count // wide, turn_keys, 0)

    @pl.when(core == 0)
    def _():
        pl.semaphore_wait(barrier, 30)
        pl.semaphore_signal(told, inc=1, device_id=(ctx, odd), device_id_type=MESH)

    wait(plane.at[pl.ds(0, 62), pl.ds(0, ROWS)], recv_sem.at[0])
    total = plane[0:16, 0:ROWS, :]
    for yy in range(1, NY):
        total = total + plane[yy * 16 : yy * 16 + 16, 0:ROWS, :]
    line[:, 0:ROWS, :] = total

    @pl.when(core == 1)
    def _():
        pl.semaphore_wait(told, 1)

    for zz in line_peers:
        copy(line.at[zz, pl.ds(0, ROWS)], part.at[z, pl.ds(0, ROWS)], 1, (y * NZ + zz, head)).start()
    part[z, 0:ROWS, :] = line[z, 0:ROWS, :]

    load_v.wait()

    def scale_values(t, _):
        turned = v_in[0, pl.ds(t * wide, wide), :].astype(F32).T
        squares = jnp.sum(turned * turned, axis=0, keepdims=True)
        scale[:, pl.ds(t * wide, wide)] = jnp.sqrt(squares / DH + 1e-06)
        return 0

    lax.fori_loop(0, key_count // wide, scale_values, 0)

    wait(part.at[pl.ds(0, 15), pl.ds(0, ROWS)], recv_sem.at[1])
    total = part[0, 0:ROWS, :]
    for zz in range(1, NZ):
        total = total + part[zz, 0:ROWS, :]
    mine = y * 16 + z
    full[mine, 0:ROWS, :] = total

    def along_z(dz):
        return y * NZ + lax.rem(z + dz, NZ)

    here = full.at[mine, pl.ds(0, ROWS)]
    for dz in FAR:
        copy(here, here, 2, (along_z(dz), head)).start()
    for dz in NEAR:
        copy(here, here, 3, (along_z(dz), head)).start()

    def pass_on(dz, phase):
        there = full.at[along_z(dz), pl.ds(0, 8)]
        for dy in (2, 1, 3):
            copy(there, there, phase, (lax.rem(y + dy, NY) * NZ + z, head)).start()

    pass_on(0, 4)
    wait(full.at[pl.ds(0, len(NEAR)), pl.ds(0, ROWS)], recv_sem.at[3])
    for dz in NEAR:
        pass_on(dz, 4)
    wait(full.at[pl.ds(0, len(FAR)), pl.ds(0, ROWS)], recv_sem.at[2])
    for dz in FAR:
        pass_on(dz, 5)

    base = lax.div(z, 2)
    order = [lax.rem(base + k, REP) for k in ORDER]
    extra = jnp.concatenate(
        [full[y * 16 + 2 * r + h, 8:9, :] for r in order for h in range(2)], axis=0
    ) * (1.0 / (query_count * NY * NZ))
    columns = extra.T
    linear_rows = split_two(extra * (1.0 / math.sqrt(DH)))

    def weigh(p, at):
        r = order[p]
        quarters = [full[q * 16 + 2 * r + h, 0:8, :] for q in range(NY) for h in range(2)]
        moments = jnp.concatenate(quarters, axis=0) * (1.0 / (query_count * NY * NZ))
        center = extra[2 * p : 2 * p + 1, :]
        up = columns[0:HALF, 2 * p : 2 * p + 1]
        down = columns[HALF:DH, 2 * p : 2 * p + 1]
        diagonal = columns[0:HALF, 2 * p + 1 : 2 * p + 2]
        below = lane < row
        value = moments - jnp.where(below, down * pltpu.roll(center, HALF, 1), up * center)
        value = value * (1.0 / (2.0 * DH))
        corner = (diagonal - down * down) * (1.0 / (2.0 * DH))
        on = lane == row
        upper = jnp.where(below, 0.0, jnp.where(on, value, 2.0 * value))
        lower = jnp.where(below, 2.0 * value, jnp.where(on, corner, 0.0))
        for block in (upper, pltpu.roll(lower, HALF, 1)):
            high, low = split_two(block)
            weights[at : at + HALF, 0:DH] = high
            weights[at : at + HALF, DH : 2 * DH] = low
            at += HALF

    tile = 512

    def score(members, at):
        end = at + len(members) * DH
        for i, p in enumerate(members):
            weigh(p, at + i * DH)
        weights[end : end + 16, 0:DH] = linear_rows[0]
        weights[end : end + 16, DH : 2 * DH] = linear_rows[1]
        for t in range(key_count // tile):
            keys = keys_t[:, t * tile : (t + 1) * tile]
            keys_f32 = keys[0:DH].astype(F32)
            projected = jnp.dot(weights[at : end + 16, :], keys, preferred_element_type=F32)
            for i, p in enumerate(members):
                quadratic = jnp.sum(
                    projected[i * DH : (i + 1) * DH] * keys_f32, axis=0, keepdims=True
                )
                linear = projected[end - at + 2 * p : end - at + 2 * p + 1]
                expo[p : p + 1, t * tile : (t + 1) * tile] = quadratic + linear

    near_heads, far_heads = range(0, 5), range(5, REP)
    wait(full.at[pl.ds(0, 3 * (1 + len(NEAR))), pl.ds(0, 8)], recv_sem.at[4])
    score(near_heads, 0)
    wait(full.at[pl.ds(0, 3 * len(FAR)), pl.ds(0, 8)], recv_sem.at[5])
    score(far_heads, 5 * DH + 16)

    exponent = expo[...]
    peak = jnp.max(exponent, axis=1, keepdims=True)
    grown = jnp.exp(exponent - peak)
    expo[...] = grown
    local = jnp.sum(grown, axis=1, keepdims=True)
    row8 = lax.broadcasted_iota(jnp.int32, (REP, DH), 0)
    lane8 = lax.broadcasted_iota(jnp.int32, (REP, DH), 1)
    place = jnp.where(row8 < 3, row8, jnp.where(row8 < 5, row8 + 3, row8 - 2))
    place = lax.rem(place + base, REP)
    note = jnp.where(lane8 == place, peak, jnp.where(lane8 == place + REP, local, 0.0))
    mass[pl.ds(ctx, 1), :] = jnp.sum(note, axis=0, keepdims=True)
    for dz in FAR_FIRST + (0,):
        for dy in (2, 1, 3, 0):
            if (dy, dz) != (0, 0):
                here = mass.at[pl.ds(ctx, 1)]
                copy(here, here, 6, (lax.rem(y + dy, NY) * NZ + lax.rem(z + dz, NZ), head)).start()
    wait(mass.at[pl.ds(0, 63)], recv_sem.at[6])
    notes = mass[...]
    highest = jnp.max(notes, axis=0, keepdims=True)
    sums = pltpu.roll(notes, DH - REP, 1)
    inside = lax.broadcasted_iota(jnp.int32, notes.shape, 1) < REP
    terms = jnp.where(inside, sums * jnp.exp(jnp.where(inside, notes - highest, 0.0)), 0.0)
    denominator = jnp.sum(terms, axis=0, keepdims=True)
    pick = lane8 == place
    highest_col = jnp.sum(jnp.where(pick, highest, 0.0), axis=1, keepdims=True)
    denominator_col = jnp.sum(jnp.where(pick, denominator, 0.0), axis=1, keepdims=True)
    factor = jnp.exp(peak - highest_col) / denominator_col
    share = jnp.sum(expo[...] * factor, axis=0, keepdims=True)
    out_ref[...] = share * scale[...] * (key_count * NY * NZ / REP)

    wait(plane.at[pl.ds(0, 62), pl.ds(0, ROWS)], send_sem.at[0])
    wait(part.at[pl.ds(0, 15), pl.ds(0, ROWS)], send_sem.at[1])
    wait(full.at[pl.ds(0, len(FAR)), pl.ds(0, ROWS)], send_sem.at[2])
    wait(full.at[pl.ds(0, len(NEAR)), pl.ds(0, ROWS)], send_sem.at[3])
    wait(full.at[pl.ds(0, 3 * (1 + len(NEAR))), pl.ds(0, 8)], send_sem.at[4])
    wait(full.at[pl.ds(0, 3 * len(FAR)), pl.ds(0, 8)], send_sem.at[5])
    wait(mass.at[pl.ds(0, 63)], send_sem.at[6])


def local(query_rows, key_rows, value_rows):
    query_count = query_rows.shape[1]
    key_count = key_rows.shape[1]
    any_space = pl.BlockSpec(memory_space=pltpu.HBM)
    return pl.pallas_call(
        functools.partial(kernel, query_count, key_count),
        out_shape=jax.ShapeDtypeStruct((1, key_count), F32),
        in_specs=[any_space] * 3,
        out_specs=pl.BlockSpec(memory_space=pltpu.VMEM),
        scratch_shapes=[
            pltpu.VMEM(query_rows.shape, BF16),
            pltpu.VMEM(key_rows.shape, BF16),
            pltpu.VMEM(value_rows.shape, BF16),
            pltpu.VMEM((query_count * NH, DH), F32),
            pltpu.VMEM((NH, NY, 2, 16, DH), F32),
            pltpu.VMEM((NY * 16, 16, DH), F32),
            pltpu.VMEM((NZ, 16, DH), F32),
            pltpu.VMEM((NZ, 16, DH), F32),
            pltpu.VMEM((NY * 16, 16, DH), F32),
            pltpu.VMEM((REP * DH + 32, 2 * DH), BF16),
            pltpu.VMEM((2 * DH, key_count), BF16),
            pltpu.VMEM((1, key_count), F32),
            pltpu.VMEM((REP, key_count), F32),
            pltpu.VMEM((NY * NZ, DH), F32),
            pltpu.SemaphoreType.DMA((3,)),
            pltpu.SemaphoreType.DMA((7,)),
            pltpu.SemaphoreType.DMA((7,)),
            pltpu.SemaphoreType.REGULAR,
        ],
        compiler_params=pltpu.CompilerParams(
            collective_id=0, has_side_effects=True, vmem_limit_bytes=62 << 20
        ),
    )(query_rows, key_rows, value_rows)


def solution(mesh):
    in_specs = (P("head", "ctx", None, None), P("head", "ctx", None), P("head", "ctx", None))
    return jax.shard_map(
        local, mesh=mesh, in_specs=in_specs, out_specs=P("head", "ctx"), check_vma=False
    )
```

```python
import functools
import math

import jax
import jax.numpy as jnp
from jax import lax
from jax.experimental import pallas as pl
from jax.experimental.pallas import tpu as pltpu
from jax.sharding import PartitionSpec as P

MESH = pl.DeviceIdType.MESH
F32 = jnp.float32
BF16 = jnp.bfloat16

NY, NZ, NH = 4, 16, 8
DH = 128
HALF = DH // 2
REP = 8
ROWS = 9
FAR_FIRST = (8, 7, 9, 6, 10, 5, 11, 4, 12, 3, 13, 2, 14, 1, 15)
FAR = (8, 7, 9, 6, 10)
NEAR = (5, 11, 4, 12, 3, 13, 2, 14, 1, 15)
PLANE = sorted(
    ((dy, dx) for dy in range(4) for dx in range(4)),
    key=lambda d: -(min(d[0], 4 - d[0]) + min(d[1], 4 - d[1])),
)


def split_two(value):
    high = value.astype(BF16)
    low = (value - high.astype(F32)).astype(BF16)
    return high, low


def kernel(
    query_count, key_count,
    q_hbm, k_hbm, v_hbm, out_ref,
    q_in, k_in, v_in, q_f32, packed, plane, line, part, full, columns, weights, keys_t, scale,
    expo, mass, in_sem, send_sem, recv_sem, told,
):
    ctx = lax.axis_index("ctx")
    head = lax.axis_index("head")
    y = lax.div(ctx, NZ)
    z = lax.rem(ctx, NZ)

    load_q = pltpu.make_async_copy(q_hbm, q_in, in_sem.at[0])
    load_k = pltpu.make_async_copy(k_hbm, k_in, in_sem.at[1])
    load_v = pltpu.make_async_copy(v_hbm, v_in, in_sem.at[2])
    load_q.start()

    plane_peers = [
        (lax.rem(y + dy, NY), lax.rem(head + 2 * dx + dc, NH))
        for dy, dx in PLANE
        for dc in range(2)
        if (dy, dx, dc) != (0, 0, 0)
    ]
    line_peers = [lax.rem(z + dz, NZ) for dz in FAR_FIRST]

    barrier = pltpu.get_barrier_semaphore()
    core = lax.rem(head, 2)
    even = head - core
    odd = even + 1

    def greet(device):
        pl.semaphore_signal(barrier, inc=1, device_id=device, device_id_type=MESH)

    for dy, dx in PLANE:
        if (dy, dx) != (0, 0):
            greet((lax.rem(y + dy, NY) * NZ + z, lax.rem(odd + 2 * dx, NH)))
    for zz in line_peers:
        greet((y * NZ + zz, even))

    @pl.when(core == 0)
    def _():
        greet((ctx, odd))

    load_q.wait()
    load_k.start()
    load_v.start()
    step = 64

    def widen(t, _):
        rows = q_in[0, pl.ds(t * step, step)].astype(F32)
        q_f32[pl.ds(t * step * NH, step * NH), :] = rows.reshape(step * NH, DH)
        return 0

    lax.fori_loop(0, query_count // step, widen, 0)
    row = lax.broadcasted_iota(jnp.int32, (HALF, DH), 0)
    lane = lax.broadcasted_iota(jnp.int32, (HALF, DH), 1)
    for g in range(NH):
        rows = q_f32[pl.ds(g, query_count, stride=NH), :]
        first = jnp.sum(rows, axis=0, keepdims=True)
        narrow = rows.astype(BF16)
        second = lax.dot_general(
            narrow, narrow, (((0,), (0,)), ((), ())), preferred_element_type=F32
        )
        top = second[:HALF]
        bottom = pltpu.roll(second[HALF:], HALF, 1)
        both = jnp.where(lane < row, bottom, top)
        diagonal = jnp.sum(jnp.where(lane == row, bottom, 0.0), axis=0, keepdims=True)
        for q in range(NY):
            for h in range(2):
                at = q * 16 + h * 8
                packed[g, q, h, 0:8, :] = both[at : at + 8]
            packed[g, q, 0, 8:9, :] = first
            packed[g, q, 1, 8:9, :] = diagonal

    @pl.when(core == 1)
    def _():
        pl.semaphore_wait(barrier, 31)
        pl.semaphore_signal(told, inc=1, device_id=(ctx, even), device_id_type=MESH)

    @pl.when(core == 0)
    def _():
        pl.semaphore_wait(told, 1)

    def copy(src, dst, phase, device):
        return pltpu.make_async_remote_copy(
            src_ref=src, dst_ref=dst, send_sem=send_sem.at[phase], recv_sem=recv_sem.at[phase],
            device_id=device, device_id_type=MESH,
        )

    def wait(ref, sem):
        pltpu.make_async_copy(ref, ref, sem).wait()

    for yy, hh in plane_peers:
        copy(
            packed.at[hh, yy, :, pl.ds(0, ROWS)],
            plane.at[pl.ds(y * 16 + 2 * head, 2), pl.ds(0, ROWS)],
            0, (yy * NZ + z, hh),
        ).start()
    plane[pl.ds(y * 16 + 2 * head, 2), 0:ROWS, :] = packed[head, y, :, 0:ROWS, :]

    load_k.wait()
    wide = 512

    def turn_keys(t, _):
        turned = k_in[0, pl.ds(t * wide, wide), :].astype(F32).T.astype(BF16)
        keys_t[0:DH, pl.ds(t * wide, wide)] = turned
        keys_t[DH : 2 * DH, pl.ds(t * wide, wide)] = turned
        return 0

    lax.fori_loop(0, key_count // wide, turn_keys, 0)

    @pl.when(core == 0)
    def _():
        pl.semaphore_wait(barrier, 30)
        pl.semaphore_signal(told, inc=1, device_id=(ctx, odd), device_id_type=MESH)

    wait(plane.at[pl.ds(0, 62), pl.ds(0, ROWS)], recv_sem.at[0])
    total = plane[0:16, 0:ROWS, :]
    for yy in range(1, NY):
        total = total + plane[yy * 16 : yy * 16 + 16, 0:ROWS, :]
    line[:, 0:ROWS, :] = total

    @pl.when(core == 1)
    def _():
        pl.semaphore_wait(told, 1)

    for zz in line_peers:
        copy(line.at[zz, pl.ds(0, ROWS)], part.at[z, pl.ds(0, ROWS)], 1, (y * NZ + zz, head)).start()
    part[z, 0:ROWS, :] = line[z, 0:ROWS, :]

    load_v.wait()

    def scale_values(t, _):
        turned = v_in[0, pl.ds(t * wide, wide), :].astype(F32).T
        squares = jnp.sum(turned * turned, axis=0, keepdims=True)
        values = jnp.sqrt(squares / DH + 1e-06) * (key_count * NY * NZ / REP)
        scale[:, pl.ds(t * wide, wide)] = values
        return 0

    lax.fori_loop(0, key_count // wide, scale_values, 0)

    wait(part.at[pl.ds(0, 15), pl.ds(0, ROWS)], recv_sem.at[1])
    total = part[0, 0:ROWS, :]
    for zz in range(1, NZ):
        total = total + part[zz, 0:ROWS, :]
    mine = y * 16 + z
    full[mine, 0:ROWS, :] = total

    def along_z(dz):
        return y * NZ + lax.rem(z + dz, NZ)

    here = full.at[mine, pl.ds(0, ROWS)]
    for dz in FAR:
        copy(here, here, 2, (along_z(dz), head)).start()
    for dz in NEAR:
        copy(here, here, 3, (along_z(dz), head)).start()

    def pass_on(dz, phase):
        there = full.at[along_z(dz), pl.ds(0, 8)]
        for dy in (2, 1, 3):
            copy(there, there, phase, (lax.rem(y + dy, NY) * NZ + z, head)).start()

    pass_on(0, 4)
    wait(full.at[pl.ds(0, len(NEAR)), pl.ds(0, ROWS)], recv_sem.at[3])
    for dz in NEAR:
        pass_on(dz, 4)
    wait(full.at[pl.ds(0, len(FAR)), pl.ds(0, ROWS)], recv_sem.at[2])
    for dz in FAR:
        pass_on(dz, 5)

    extra = full[pl.ds(y * 16, 16), 8, :] * (1.0 / (query_count * NY * NZ))
    columns[:, 0:16] = extra.T
    row16 = lax.broadcasted_iota(jnp.int32, (16, DH), 0)
    lane16 = lax.broadcasted_iota(jnp.int32, (16, DH), 1)

    def quarter(dq):
        return lax.rem(y + dq, NY)

    def sixteen(start):
        return pl.ds(pl.multiple_of(start, 16), 16)

    def weigh(dq, at):
        q = quarter(dq)
        ups = columns[sixteen(q * 16), 0:16]
        downs = columns[sixteen(HALF + q * 16), 0:16]
        below = lane16 < row16 + q * 16
        on = lane16 == row16 + q * 16
        for r in range(REP):
            moments = jnp.concatenate(
                [full[q * 16 + 2 * r + h, 0:8, :] for h in range(2)], axis=0
            ) * (1.0 / (query_count * NY * NZ))
            center = extra[2 * r : 2 * r + 1, :]
            up = ups[:, 2 * r : 2 * r + 1]
            down = downs[:, 2 * r : 2 * r + 1]
            diagonal = ups[:, 2 * r + 1 : 2 * r + 2]
            value = moments - jnp.where(below, down * pltpu.roll(center, HALF, 1), up * center)
            value = value * (1.0 / (2.0 * DH))
            corner = (diagonal - down * down) * (1.0 / (2.0 * DH))
            upper = jnp.where(below, 0.0, jnp.where(on, value, 2.0 * value))
            lower = jnp.where(below, 2.0 * value, jnp.where(on, corner, 0.0))
            for start, block in ((at, upper), (at + REP * 16, pltpu.roll(lower, HALF, 1))):
                high, low = split_two(block)
                start += r * 16
                weights[start : start + 16, 0:DH] = high
                weights[start : start + 16, DH : 2 * DH] = low

    tile = 512
    tiles = [pl.ds(t * tile, tile) for t in range(key_count // tile)]
    rows_of = 2 * REP * 16

    def score(quarters, at, end, span):
        keys = keys_t[:, span]
        projected = jnp.dot(weights[at:end, :], keys, preferred_element_type=F32)
        totals = [0.0] * REP
        for i, dq in enumerate(quarters):
            for half in range(2):
                some = keys_t[sixteen(half * HALF + quarter(dq) * 16), span].astype(F32)
                for r in range(REP):
                    start = i * rows_of + (half * REP + r) * 16
                    totals[r] = totals[r] + projected[start : start + 16] * some
        return [jnp.sum(v, axis=0, keepdims=True) for v in totals], projected

    weigh(0, 0)
    high, low = split_two(extra * (1.0 / math.sqrt(DH)))
    weights[rows_of : rows_of + 16, 0:DH] = high
    weights[rows_of : rows_of + 16, DH : 2 * DH] = low
    for span in tiles:
        totals, projected = score((0,), 0, rows_of + 16, span)
        for r in range(REP):
            linear = projected[rows_of + 2 * r : rows_of + 2 * r + 1]
            expo[r : r + 1, span] = totals[r] + linear

    wait(full.at[pl.ds(0, 3 * (1 + len(NEAR))), pl.ds(0, 8)], recv_sem.at[4])
    wait(full.at[pl.ds(0, 3 * len(FAR)), pl.ds(0, 8)], recv_sem.at[5])
    for dq in range(1, NY):
        weigh(dq, rows_of * dq + 16)
    tops, sums = [], []
    for span in tiles:
        totals, _ = score((1, 2, 3), rows_of + 16, NY * rows_of + 16, span)
        for r in range(REP):
            expo[r : r + 1, span] = expo[r : r + 1, span] + totals[r]
        pieces = jnp.split(expo[:, span], tile // DH, axis=1)
        top = functools.reduce(jnp.maximum, pieces)
        pieces = [jnp.exp(piece - top) for piece in pieces]
        expo[:, span] = jnp.concatenate(pieces, axis=1)
        tops.append(top)
        sums.append(functools.reduce(jnp.add, pieces))

    peak = jnp.max(functools.reduce(jnp.maximum, tops), axis=1, keepdims=True)
    lifts = [jnp.exp(top - peak) for top in tops]
    local = jnp.sum(sum(v * f for v, f in zip(sums, lifts)), axis=1, keepdims=True)
    row8 = lax.broadcasted_iota(jnp.int32, (REP, DH), 0)
    lane8 = lax.broadcasted_iota(jnp.int32, (REP, DH), 1)
    note = jnp.where(lane8 == row8, peak, jnp.where(lane8 == row8 + REP, local, 0.0))
    mass[pl.ds(ctx, 1), :] = jnp.sum(note, axis=0, keepdims=True)
    for dz in FAR_FIRST + (0,):
        for dy in (2, 1, 3, 0):
            if (dy, dz) != (0, 0):
                here = mass.at[pl.ds(ctx, 1)]
                copy(here, here, 6, (lax.rem(y + dy, NY) * NZ + lax.rem(z + dz, NZ), head)).start()
    wait(mass.at[pl.ds(0, 63)], recv_sem.at[6])
    notes = mass[...]
    highest = jnp.max(notes, axis=0, keepdims=True)
    sums = pltpu.roll(notes, DH - REP, 1)
    inside = lax.broadcasted_iota(jnp.int32, notes.shape, 1) < REP
    terms = jnp.where(inside, sums * jnp.exp(jnp.where(inside, notes - highest, 0.0)), 0.0)
    denominator = jnp.sum(terms, axis=0, keepdims=True)
    pick = lane8 == row8
    highest_col = jnp.sum(jnp.where(pick, highest, 0.0), axis=1, keepdims=True)
    denominator_col = jnp.sum(jnp.where(pick, denominator, 0.0), axis=1, keepdims=True)
    factor = jnp.exp(peak - highest_col) / denominator_col
    for span, lift in zip(tiles, lifts):
        weight = jnp.concatenate([lift * factor] * (tile // DH), axis=1)
        share = jnp.sum(expo[:, span] * weight, axis=0, keepdims=True)
        out_ref[:, span] = share * scale[:, span]

    wait(plane.at[pl.ds(0, 62), pl.ds(0, ROWS)], send_sem.at[0])
    wait(part.at[pl.ds(0, 15), pl.ds(0, ROWS)], send_sem.at[1])
    wait(full.at[pl.ds(0, len(FAR)), pl.ds(0, ROWS)], send_sem.at[2])
    wait(full.at[pl.ds(0, len(NEAR)), pl.ds(0, ROWS)], send_sem.at[3])
    wait(full.at[pl.ds(0, 3 * (1 + len(NEAR))), pl.ds(0, 8)], send_sem.at[4])
    wait(full.at[pl.ds(0, 3 * len(FAR)), pl.ds(0, 8)], send_sem.at[5])
    wait(mass.at[pl.ds(0, 63)], send_sem.at[6])


def local(query_rows, key_rows, value_rows):
    query_count = query_rows.shape[1]
    key_count = key_rows.shape[1]
    any_space = pl.BlockSpec(memory_space=pltpu.HBM)
    return pl.pallas_call(
        functools.partial(kernel, query_count, key_count),
        out_shape=jax.ShapeDtypeStruct((1, key_count), F32),
        in_specs=[any_space] * 3,
        out_specs=pl.BlockSpec(memory_space=pltpu.VMEM),
        scratch_shapes=[
            pltpu.VMEM(query_rows.shape, BF16),
            pltpu.VMEM(key_rows.shape, BF16),
            pltpu.VMEM(value_rows.shape, BF16),
            pltpu.VMEM((query_count * NH, DH), F32),
            pltpu.VMEM((NH, NY, 2, 16, DH), F32),
            pltpu.VMEM((NY * 16, 16, DH), F32),
            pltpu.VMEM((NZ, 16, DH), F32),
            pltpu.VMEM((NZ, 16, DH), F32),
            pltpu.VMEM((NY * 16, 16, DH), F32),
            pltpu.VMEM((DH, DH), F32),
            pltpu.VMEM((REP * DH + 16, 2 * DH), BF16),
            pltpu.VMEM((2 * DH, key_count), BF16),
            pltpu.VMEM((1, key_count), F32),
            pltpu.VMEM((REP, key_count), F32),
            pltpu.VMEM((NY * NZ, DH), F32),
            pltpu.SemaphoreType.DMA((3,)),
            pltpu.SemaphoreType.DMA((7,)),
            pltpu.SemaphoreType.DMA((7,)),
            pltpu.SemaphoreType.REGULAR,
        ],
        compiler_params=pltpu.CompilerParams(
            collective_id=0, has_side_effects=True, vmem_limit_bytes=53 << 20
        ),
    )(query_rows, key_rows, value_rows)


def solution(mesh):
    in_specs = (P("head", "ctx", None, None), P("head", "ctx", None), P("head", "ctx", None))
    return jax.shard_map(
        local, mesh=mesh, in_specs=in_specs, out_specs=P("head", "ctx"), check_vma=False
    )
```
